32 devices in a mesh: px: 8 (over z, y), py: 4 (over x, core).
Axes of the slice: x: 2, y: 2, z: 4, core: 2. Of those that a mesh axis runs over, the one named last changes fastest.
Arguments:
- right_sides: bfloat16 [16, 2048, 512], P('px', 'py'), may hold values from -6 to 6
- tree_order: int32 [16, 2048], P('px', 'py'), may hold values from 0 to 2047, as said below
- dense_blocks: bfloat16 [16, 2048, 2048], P('px', 'py'), may hold values from -0.125 to 0.125
- basis_out: bfloat16 [16, 2048, 256], P('px', 'py'), may hold values from -0.375 to 0.375
- basis_in: bfloat16 [16, 2048, 256], P('px', 'py'), may hold values from -0.125 to 0.125
- leaf_transfer: bfloat16 [16, 256, 256], P('px'), may hold values from -0.375 to 0.375
- leaf_coupling: bfloat16 [16, 256, 256], P('px'), may hold values from -0.09375 to 0.09375
- chain_transfer: bfloat16 [8, 3, 256, 256], P('px'), as said below
- chain_coupling: bfloat16 [8, 3, 256, 256], P('px'), as said below
Outputs:
- kernel_product: float32 [16, 2048, 512], P('px', 'py')
The draws below stay inside these ranges and needn't reach their ends.
Inputs may be any that keep to these rules, and one draw needn't show every extreme that they name: `tree_order`: each row is a permutation, and each aligned block of 512 entries holds exactly the positions of that block. `chain_transfer`: entry [p, k] is the same matrix for all p with the same p // 2**k. `chain_coupling`: entry [p, k] is the same matrix for all p with the same p // 2**k.
All inputs are finite; a program needn't handle non-finite values.
Results may differ from the reference program's by a relative error of at most 0.0019.
Values may be sent and summed in bfloat16 or wider, within the bound.
A program may use at most 64 MiB of HBM per device.

```python
import jax
import jax.numpy as jnp
from jax import lax

LEAF = 2048
R = 256
RHS = 512
LEAVES = 16
PTS_DEV = 512
LEVELS = 3
N_PX = 8


def replicate_chain(sample):
    owners = jnp.arange(N_PX, dtype=jnp.int32)
    copies = [sample[jnp.left_shift(jnp.right_shift(owners, height), height), height] for height in range(LEVELS)]
    return jnp.stack(copies, axis=1).astype(jnp.bfloat16)


def draw_tree_order(key, part):
    key = jax.random.fold_in(key, 11)
    blocks = LEAVES * (LEAF // PTS_DEV)
    shuffles = jax.vmap(lambda single: jax.random.permutation(single, PTS_DEV))(jax.random.split(key, blocks))
    offsets = jnp.arange(blocks, dtype=jnp.int32) % (LEAF // PTS_DEV) * PTS_DEV
    return (shuffles.astype(jnp.int32) + offsets[:, None]).reshape(LEAVES, LEAF)


def draw_chain_transfer(key, part):
    key = jax.random.fold_in(key, 12)
    extent = (N_PX, LEVELS, R, R)
    sample = jax.random.normal(key, extent, jnp.float32)
    return replicate_chain(sample * R ** (-0.5))


def draw_chain_coupling(key, part):
    key = jax.random.fold_in(key, 13)
    extent = (N_PX, LEVELS, R, R)
    sample = jax.random.normal(key, extent, jnp.float32)
    return replicate_chain(sample * (0.25 * R ** (-0.5)))


def level_of(stream_key, dims, pieces, low, high):
    level = 1.0
    for position, blocks in pieces:
        draws = jax.random.uniform(jax.random.fold_in(jax.random.fold_in(stream_key, 6), position), (blocks,), jnp.float32, low / len(pieces), high / len(pieces))
        level = level * jnp.repeat(jnp.exp(draws), dims[position] // blocks).reshape((-1,) + (1,) * (len(dims) - 1 - position))
    return level


def noise(own_key, dims, spread, reach, cuts=(), kind=jnp.bfloat16):
    entries = spread * jax.random.normal(own_key, dims, jnp.float32)
    if cuts:
        entries = entries * level_of(own_key, dims, cuts, -0.22, 0.18)
    return jnp.clip(entries, -reach, reach).astype(kind)


def setup_inputs(seed: int = 0) -> dict:
    key_list = jax.random.split(jax.random.key(seed), 10)
    right_sides = noise(key_list[0], (LEAVES, LEAF, RHS), 1.0, 6.0, ((0, 8), (1, 4)))
    tree_order = draw_tree_order(jax.random.fold_in(key_list[9], 71), 0)
    dense_blocks = noise(key_list[2], (LEAVES, LEAF, LEAF), LEAF ** -0.5, 0.125, ((0, 8), (1, 4)))
    basis_out = noise(key_list[3], (LEAVES, LEAF, R), R ** -0.5, 0.375, ((0, 8), (1, 4)))
    basis_in = noise(key_list[4], (LEAVES, LEAF, R), LEAF ** -0.5, 0.125, ((0, 8), (1, 4)))
    leaf_transfer = noise(key_list[5], (LEAVES, R, R), R ** -0.5, 0.375, ((0, 8),))
    leaf_coupling = noise(key_list[6], (LEAVES, R, R), (0.25 / R ** 0.5), 0.09375, ((0, 8),))
    chain_transfer = draw_chain_transfer(jax.random.fold_in(key_list[9], 71), 0)
    chain_coupling = draw_chain_coupling(jax.random.fold_in(key_list[9], 71), 0)
    return {"right_sides": right_sides, "tree_order": tree_order, "dense_blocks": dense_blocks, "basis_out": basis_out, "basis_in": basis_in, "leaf_transfer": leaf_transfer, "leaf_coupling": leaf_coupling, "chain_transfer": chain_transfer, "chain_coupling": chain_coupling}


HIGHEST = lax.Precision.HIGHEST


def pick_rows(values, indices):
    return values[indices]


def place_rows(values, indices):
    return jnp.zeros_like(values).at[indices].set(values)


def lift(weight, values):
    return jnp.einsum("nab,nar->nbr", weight.astype(jnp.float32), values, precision=HIGHEST)


def lower(weight, values):
    return jnp.einsum("nab,nbr->nar", weight.astype(jnp.float32), values, precision=HIGHEST)


def paired(values):
    amount = values.shape[0]
    return values.reshape((amount // 2, 2) + values.shape[1:])[:, ::-1].reshape(values.shape)


def leaf_terms(operands):
    dense, permuted, inward = operands
    nearby = jnp.dot(dense, permuted, preferred_element_type=jnp.float32)
    coefficients = jnp.dot(inward.T, permuted, preferred_element_type=jnp.float32)
    return nearby, coefficients


def reference(right_sides, tree_order, dense_blocks, basis_out, basis_in, leaf_transfer, leaf_coupling, chain_transfer, chain_coupling):
    permuted = jax.vmap(pick_rows)(right_sides, tree_order)
    nearby, coefficients = lax.map(leaf_terms, (dense_blocks, permuted, basis_in))
    lifted = lift(leaf_transfer, coefficients)
    subtree = lifted[0::2] + lifted[1::2]
    by_height = []
    for height in range(LEVELS):
        by_height.append(subtree)
        if height + 1 < LEVELS:
            lifted = lift(chain_transfer[::2 ** height, height], subtree)
            subtree = lifted[0::2] + lifted[1::2]
    descend = jnp.zeros((1, R, RHS), jnp.float32)
    for height in reversed(range(LEVELS)):
        repeated = jnp.repeat(descend, 2, axis=0)
        descend = lower(chain_coupling[::2 ** height, height], paired(by_height[height])) + lower(chain_transfer[::2 ** height, height], repeated)
    repeated = jnp.repeat(descend, 2, axis=0)
    leaf_down = lower(leaf_coupling, paired(coefficients)) + lower(leaf_transfer, repeated)
    leaf_down = lax.optimization_barrier(leaf_down.astype(jnp.bfloat16)).astype(jnp.float32)
    distant = jnp.einsum("npk,nkr->npr", basis_out.astype(jnp.float32), leaf_down, precision=HIGHEST)
    result_tree = nearby + distant
    return jax.vmap(place_rows)(result_tree, tree_order)
```

```python
import functools

import jax
import jax.numpy as jnp
from jax import lax
from jax.experimental import pallas as pl
from jax.experimental.pallas import tpu as pltpu
from jax.sharding import PartitionSpec as P

MESH = pl.DeviceIdType.MESH
BF16 = jnp.bfloat16
F32 = jnp.float32
CHUNKS = 4


def dot(a, b):
    return jnp.dot(a, b, preferred_element_type=F32)


def dot_nt(a, b):
    return lax.dot_general(a, b, (((1,), (1,)), ((), ())), preferred_element_type=F32)


def dot_tn(a, b):
    return lax.dot_general(a, b, (((0,), (0,)), ((), ())), preferred_element_type=F32)


def halves(v):
    high = v.astype(BF16)
    low = (v - high.astype(F32)).astype(BF16)
    return jnp.concatenate([high, low], axis=0)


def lift(v, w):
    t = dot(halves(v), w)
    n = v.shape[0]
    return t[:n] + t[n:]


def lower(v, w):
    t = dot_nt(halves(v), w)
    n = v.shape[0]
    return t[:n] + t[n:]


def kernel(
    npx,
    npy,
    rs_in,
    order,
    dense_in,
    bout_in,
    bin_in,
    lt_in,
    lc_in,
    ct_in,
    cc_in,
    out,
    rs,
    dense,
    bout,
    bin_,
    lt,
    lc,
    ct,
    cc,
    onehot,
    moved,
    bmoved,
    coef,
    near_in,
    part,
    far_in,
    g,
    near,
    wsib,
    ssend,
    srecv,
    ldg,
    result,
    load_sem,
    out_sem,
    w_sem,
    near_sem,
    far_sem,
    own_sem,
    x_sem,
    fwd_sem,
    s_sem,
    ld_sem,
    ldf_sem,
):
    levels = npx.bit_length() - 1
    nx = npy // 2
    leaves, rows, width = rs.shape
    n = width // npy
    px = lax.axis_index("px")
    py = lax.axis_index("py")
    x = py // 2
    c = py % 2
    twin = {"py": 2 * x + 1 - c}

    def chip(d):
        return lax.rem(x + d + nx, nx)

    def peer(d):
        return {"py": 2 * chip(d) + c}

    def sibling(k):
        bit = (px // 2**k) % 2
        return {"px": px + 2**k * (1 - 2 * bit)}

    def remote(src, dst, sems, index, device):
        return pltpu.make_async_remote_copy(
            src_ref=src,
            dst_ref=dst,
            send_sem=sems.at[(0,) + index],
            recv_sem=sems.at[(1,) + index],
            device_id=device,
            device_id_type=MESH,
        )

    loads = []

    def load(src, dst):
        copy = pltpu.make_async_copy(src, dst, load_sem.at[len(loads)])
        copy.start()
        loads.append(copy)
        return copy

    early = [load(bin_in, bin_), load(rs_in, rs)]
    tree_loads = [load(lt_in, lt), load(ct_in, ct), load(lc_in, lc), load(cc_in, cc)]
    bout_load = load(bout_in, bout)
    dense_loads = [
        [load(dense_in.at[l, :, pl.ds(q * rows, rows)], dense.at[l, q]) for q in range(npy)]
        for l in range(leaves)
    ]

    partners = [twin] + [peer(d) for d in range(1, nx)] + [sibling(k) for k in range(levels)]
    barrier = pltpu.get_barrier_semaphore()
    for device in partners:
        pl.semaphore_signal(barrier, inc=1, device_id=device, device_id_type=MESH)
    pl.semaphore_wait(barrier, len(partners))

    w_copies = [
        remote(ct_in.at[0, k], wsib.at[k], w_sem, (k,), sibling(k)) for k in range(levels - 1)
    ]
    for copy in w_copies:
        copy.start()

    for copy in early:
        copy.wait()
    places = lax.broadcasted_iota(jnp.int32, (rows, rows), 0)
    for l in range(leaves):
        position = order[l : l + 1, :] - py * rows
        onehot[l] = jnp.where(places == position, 1.0, 0.0).astype(BF16)
        inward = dot(onehot[l], bin_[l]).astype(BF16)
        values = dot_tn(rs[l], inward)
        for q in range(npy):
            coef[q, l] = values[q * n : (q + 1) * n]

    near_copies = {}
    for d in list(range(1, nx)) + [0]:
        copy = remote(coef.at[2 * chip(d) + 1 - c], near_in.at[d], near_sem, (d,), twin)
        copy.start()
        near_copies[d] = copy

    own_copies = []
    x_copies = {}
    step = rows // CHUNKS

    def x_copy(l, h, d):
        piece = pl.ds(h * step, step)
        return remote(
            g.at[0, 0, l, piece], g.at[0, d, l, piece], x_sem, (l, h, d - 1), peer(d)
        )

    for l in range(leaves):
        g[0, 0, l] = dot_tn(onehot[l], rs[l]).astype(BF16)
        copy = remote(g.at[0, 0, l], g.at[1, 0, l], own_sem, (l,), twin)
        copy.start()
        own_copies.append(copy)
        if l == 0:
            for d in range(1, nx):
                x_copies[0, 0, d] = x_copy(0, 0, d)
                x_copies[0, 0, d].start()

    far_copies = []
    for d in range(1, nx):
        near_copies[d].wait_recv()
        part[d] = coef[2 * chip(d) + c] + near_in[d]
        copy = remote(part.at[d], far_in.at[d], far_sem, (d,), peer(d))
        copy.start()
        far_copies.append(copy)
    near_copies[0].wait_recv()
    part[0] = coef[2 * x + c] + near_in[0]

    def multiply(l, side, d, first=False):
        q = 2 * chip(-d) + (c if side == 0 else 1 - c)
        product = dot(moved[l, q], g[side, d, l])
        near[l] = product if first else near[l] + product

    bout_load.wait()
    for l in range(leaves):
        bmoved[l] = dot(onehot[l], bout[l]).astype(BF16)
        for copy in dense_loads[l]:
            copy.wait()

        def move(q, carry, l=l):
            moved[l, q] = dot(onehot[l], dense[l, q]).astype(BF16)
            return carry

        lax.fori_loop(0, npy, move, 0)
        multiply(l, 0, 0, first=True)

    for copy in far_copies:
        copy.wait_send()
    for l in range(leaves):
        for h in range(CHUNKS):
            for d in range(1, nx):
                if (l, h, d) not in x_copies:
                    x_copies[l, h, d] = x_copy(l, h, d)
                    x_copies[l, h, d].start()

    total = part[0]
    for copy, d in zip(far_copies, range(1, nx)):
        copy.wait_recv()
        total = total + far_in[d]
    first_coef, second_coef = total[0], total[1]

    forwards = []

    def forward(l, h):
        piece = pl.ds(h * step, step)
        for d in range(1, nx):
            x_copies[l, h, d].wait_recv()
            copy = remote(
                g.at[0, d, l, piece], g.at[1, d, l, piece], fwd_sem, (l, h, d - 1), twin
            )
            copy.start()
            forwards.append(copy)

    for copy in tree_loads:
        copy.wait()
    subtree = lift(first_coef, lt[0]) + lift(second_coef, lt[1])
    coupled = []
    s_copies = []
    for k in range(levels):
        ssend[k] = subtree
        copy = remote(ssend.at[k], srecv.at[k], s_sem, (k,), sibling(k))
        copy.start()
        s_copies.append(copy)
        if k == 0:
            first_down = lower(second_coef, lc[0])
            second_down = lower(first_coef, lc[1])
        else:
            coupled.append(lower(srecv[k - 1], cc[0, k - 1]))
        if k < levels - 1:
            own = lift(subtree, ct[0, k])
        if k == 0:
            for l in range(leaves):
                own_copies[l].wait_recv()
                multiply(l, 1, 0)
        if k == levels - 1:
            forward(0, 0)
            forward(0, 1)
        copy.wait_recv()
        if k < levels - 1:
            w_copies[k].wait_recv()
            subtree = own + lift(srecv[k], wsib[k])

    descend = lower(srecv[levels - 1], cc[0, levels - 1])
    for k in reversed(range(levels - 1)):
        descend = coupled[k] + lower(descend, ct[0, k])
    ldg[py, 0] = (first_down + lower(descend, lt[0])).astype(BF16)
    ldg[py, 1] = (second_down + lower(descend, lt[1])).astype(BF16)

    ld_copies = []
    for d in range(1, nx):
        ld_copies.append(remote(ldg.at[py], ldg.at[py], ld_sem, (d,), peer(d)))
    ld_twin = remote(ldg.at[py], ldg.at[py], ld_sem, (0,), twin)
    for copy in ld_copies + [ld_twin]:
        copy.start()

    for l in range(leaves):
        for h in range(CHUNKS):
            if l > 0 or h > 1:
                forward(l, h)
        if l == 0:
            for d in range(1, nx):
                multiply(0, 0, d)

    ld_forwards = []
    for d in range(1, nx):
        ld_copies[d - 1].wait_recv()
        block = ldg.at[2 * chip(-d) + c]
        copy = remote(block, block, ldf_sem, (d - 1,), twin)
        copy.start()
        ld_forwards.append(copy)
    for d in range(1, nx):
        multiply(1, 0, d)

    per_leaf = (nx - 1) * CHUNKS
    for copy in forwards[:per_leaf]:
        copy.wait_recv()
    for d in range(1, nx):
        multiply(0, 1, d)
    for copy in forwards[per_leaf:]:
        copy.wait_recv()
    for d in range(1, nx):
        multiply(1, 1, d)
    ld_twin.wait_recv()
    for copy in ld_forwards:
        copy.wait_recv()
    out_copies = []
    for l in range(leaves):
        down = ldg[:, l].reshape(width, ldg.shape[3])
        result[l] = near[l] + dot_nt(bmoved[l], down)
        copy = pltpu.make_async_copy(result.at[l], out.at[l], out_sem.at[l])
        copy.start()
        out_copies.append(copy)

    for copy in list(near_copies.values()) + own_copies + list(x_copies.values()):
        copy.wait_send()
    for copy in w_copies + forwards + s_copies + ld_copies + [ld_twin] + ld_forwards:
        copy.wait_send()
    for copy in out_copies:
        copy.wait()


def on_device(
    right_sides,
    tree_order,
    dense_blocks,
    basis_out,
    basis_in,
    leaf_transfer,
    leaf_coupling,
    chain_transfer,
    chain_coupling,
):
    npx = lax.axis_size("px")
    npy = lax.axis_size("py")
    levels = npx.bit_length() - 1
    nx = npy // 2
    leaves, rows, width = right_sides.shape
    rank = basis_in.shape[2]
    n = width // npy
    dma = pltpu.SemaphoreType.DMA
    anywhere = pl.BlockSpec(memory_space=pl.ANY)
    inside = pl.BlockSpec(memory_space=pltpu.VMEM)
    scratch = [
        pltpu.VMEM((leaves, rows, width), BF16),
        pltpu.VMEM((leaves, npy, rows, rows), BF16),
        pltpu.VMEM((leaves, rows, rank), BF16),
        pltpu.VMEM((leaves, rows, rank), BF16),
        pltpu.VMEM(leaf_transfer.shape, BF16),
        pltpu.VMEM(leaf_coupling.shape, BF16),
        pltpu.VMEM(chain_transfer.shape, BF16),
        pltpu.VMEM(chain_coupling.shape, BF16),
        pltpu.VMEM((leaves, rows, rows), BF16),
        pltpu.VMEM((leaves, npy, rows, rows), BF16),
        pltpu.VMEM((leaves, rows, rank), BF16),
        pltpu.VMEM((npy, leaves, n, rank), F32),
        pltpu.VMEM((nx, leaves, n, rank), F32),
        pltpu.VMEM((nx, leaves, n, rank), F32),
        pltpu.VMEM((nx, leaves, n, rank), F32),
        pltpu.VMEM((2, nx, leaves, rows, width), BF16),
        pltpu.VMEM((leaves, rows, width), F32),
        pltpu.VMEM((levels - 1, rank, rank), BF16),
        pltpu.VMEM((levels, n, rank), F32),
        pltpu.VMEM((levels, n, rank), F32),
        pltpu.VMEM((npy, leaves, n, rank), BF16),
        pltpu.VMEM((leaves, rows, width), F32),
        dma((7 + leaves * npy,)),
        dma((leaves,)),
        dma((2, levels - 1)),
        dma((2, nx)),
        dma((2, nx)),
        dma((2, leaves)),
        dma((2, leaves, CHUNKS, nx - 1)),
        dma((2, leaves, CHUNKS, nx - 1)),
        dma((2, levels)),
        dma((2, nx)),
        dma((2, nx - 1)),
    ]
    return pl.pallas_call(
        functools.partial(kernel, npx, npy),
        out_shape=jax.ShapeDtypeStruct((leaves, rows, width), F32),
        in_specs=[anywhere, inside] + [anywhere] * 7,
        out_specs=anywhere,
        scratch_shapes=scratch,
        compiler_params=pltpu.CompilerParams(
            collective_id=0, has_side_effects=True, vmem_limit_bytes=48 * 2**20
        ),
    )(
        right_sides,
        tree_order,
        dense_blocks,
        basis_out,
        basis_in,
        leaf_transfer,
        leaf_coupling,
        chain_transfer,
        chain_coupling,
    )


def solution(mesh):
    in_specs = (
        P("px", "py", None),
        P("px", "py"),
        P("px", "py", None),
        P("px", "py", None),
        P("px", "py", None),
        P("px", None, None),
        P("px", None, None),
        P("px", None, None, None),
        P("px", None, None, None),
    )
    out_specs = P("px", "py", None)
    return jax.shard_map(
        on_device, mesh=mesh, in_specs=in_specs, out_specs=out_specs, check_vma=False
    )
```

```python
import functools

import jax
import jax.numpy as jnp
from jax import lax
from jax.experimental import pallas as pl
from jax.experimental.pallas import tpu as pltpu
from jax.sharding import PartitionSpec as P

MESH = pl.DeviceIdType.MESH
BF16 = jnp.bfloat16
F32 = jnp.float32
CHUNKS = 4
FIRST, SECOND, THIRD = 1, 4, 7
PARTS = 2
VMEM = 58 * 2**20


def dot(a, b):
    return jnp.dot(a, b, preferred_element_type=F32)


def dot_nt(a, b):
    return lax.dot_general(a, b, (((1,), (1,)), ((), ())), preferred_element_type=F32)


def dot_tn(a, b):
    return lax.dot_general(a, b, (((0,), (0,)), ((), ())), preferred_element_type=F32)


def halves(v):
    high = v.astype(BF16)
    low = (v - high.astype(F32)).astype(BF16)
    return jnp.concatenate([high, low], axis=0)


def lift(v, w):
    t = dot(halves(v), w)
    n = v.shape[0]
    return t[:n] + t[n:]


def lower(v, w):
    t = dot_nt(halves(v), w)
    n = v.shape[0]
    return t[:n] + t[n:]


def kernel(
    npx,
    npy,
    rs_in,
    order_in,
    dense_in,
    bout_in,
    bin_in,
    lt_in,
    lc_in,
    ct_in,
    cc_in,
    out,
    orders,
    dense,
    bout,
    bin_,
    lt,
    lc,
    ct,
    cc,
    onehot,
    moved,
    bmoved,
    coef,
    near_in,
    part,
    far_in,
    g,
    near,
    wsib,
    ssend,
    srecv,
    ldg,
    load_sem,
    out_sem,
    order_sem,
    w_sem,
    near_sem,
    far_sem,
    own_sem,
    x_sem,
    fwd_sem,
    s_sem,
    ld_sem,
    ldf_sem,
):
    levels = npx.bit_length() - 1
    nx = npy // 2
    leaves, rows, width = rs_in.shape
    n = width // npy
    px = lax.axis_index("px")
    py = lax.axis_index("py")
    x = py // 2
    c = py % 2
    twin = {"py": 2 * x + 1 - c}

    def chip(d):
        return lax.rem(x + d + nx, nx)

    def peer(d):
        return {"py": 2 * chip(d) + c}

    def sibling(k):
        bit = (px // 2**k) % 2
        return {"px": px + 2**k * (1 - 2 * bit)}

    def remote(src, dst, sems, index, device):
        return pltpu.make_async_remote_copy(
            src_ref=src,
            dst_ref=dst,
            send_sem=sems.at[(0,) + index],
            recv_sem=sems.at[(1,) + index],
            device_id=device,
            device_id_type=MESH,
        )

    loads = []
    sent = []

    def load(src, dst):
        copy = pltpu.make_async_copy(src, dst, load_sem.at[len(loads)])
        copy.start()
        loads.append(copy)
        return copy

    def send(*args):
        copy = remote(*args)
        copy.start()
        sent.append(copy)
        return copy

    order_load = load(order_in, orders.at[py])
    early = [load(bin_in, bin_), load(rs_in, g.at[0, 0])]
    tree_loads = [load(lt_in, lt), load(ct_in, ct), load(lc_in, lc), load(cc_in, cc)]
    bout_load = load(bout_in, bout)
    dense_loads = [
        [load(dense_in.at[l, :, pl.ds(q * rows, rows)], dense.at[l, q]) for q in range(npy)]
        for l in range(leaves)
    ]

    others = [{"py": lax.rem(py + d, npy)} for d in range(1, npy)]
    partners = others + [sibling(k) for k in range(levels)]
    barrier = pltpu.get_barrier_semaphore()
    for device in partners:
        pl.semaphore_signal(barrier, inc=1, device_id=device, device_id_type=MESH)

    places = lax.broadcasted_iota(jnp.int32, (rows, rows), 0)

    def selection(l, q):
        position = orders[q, pl.ds(l, 1), :] - q * rows
        return jnp.where(places == position, 1.0, 0.0).astype(BF16)

    order_load.wait()
    for l in range(leaves):
        onehot[l] = selection(l, py)
    pl.semaphore_wait(barrier, len(partners))

    step = rows // CHUNKS
    pieces = [(l, h) for l in range(leaves) for h in range(CHUNKS)]
    x_copies = {}

    def spread(wanted):
        for l, h in wanted:
            piece = pl.ds(h * step, step)
            for d in range(1, nx):
                x_copies[l, h, d] = send(
                    rs_in.at[l, piece], g.at[0, d, l, piece], x_sem, (l, h, d - 1), peer(d)
                )

    spread(pieces[:FIRST])
    order_copies = [
        send(orders.at[py], orders.at[py], order_sem, (d,), device)
        for d, device in enumerate(others)
    ]
    w_copies = [
        send(ct_in.at[0, k], wsib.at[k], w_sem, (k,), sibling(k)) for k in range(levels - 1)
    ]

    near_copies = {}
    for copy in early:
        copy.wait()
    for l in range(leaves):
        inward = dot(onehot[l], bin_[l]).astype(BF16)
        values = dot_tn(g[0, 0, l], inward)
        for q in range(npy):
            coef[q, l] = values[q * n : (q + 1) * n]
        for d in list(range(1, nx)) + [0]:
            near_copies[l, d] = send(
                coef.at[2 * chip(d) + 1 - c, l], near_in.at[d, l], near_sem, (l, d), twin
            )
    own_copies = [
        send(rs_in.at[l], g.at[1, 0, l], own_sem, (l,), twin) for l in range(leaves)
    ]

    half = n // PARTS
    spans = [pl.ds(t * half, half) for t in range(PARTS)]
    far_copies = {}
    for l in range(leaves):
        for d in range(1, nx):
            near_copies[l, d].wait_recv()
            q = 2 * chip(d) + c
            part[d, l] = coef[q, l] + near_in[d, l]
            for t in range(PARTS):
                far_copies[l, t, d] = send(
                    part.at[d, l, spans[t]],
                    far_in.at[d, l, spans[t]],
                    far_sem,
                    (l, t, d),
                    peer(d),
                )
    for l in range(leaves):
        near_copies[l, 0].wait_recv()
        part[0, l] = coef[2 * x + c, l] + near_in[0, l]

    def owner(side, d):
        return 2 * chip(-d) + (c if side == 0 else 1 - c)

    def move(l, q):
        turned = dot(onehot[l], dense[l, q]).astype(BF16)
        moved[l, q] = dot_nt(turned, selection(l, q)).astype(BF16)

    def multiply(l, side, d, first=False):
        product = dot(moved[l, owner(side, d)], g[side, d, l])
        near[l] = product if first else near[l] + product

    def multiply_piece(l, side, d, start, stop):
        q = owner(side, d)
        piece = slice(start * step, stop * step)
        return dot(moved[l, q, :, piece], g[side, d, l, piece])

    for copy in order_copies:
        copy.wait_recv()
    for l in range(leaves):
        for copy in dense_loads[l]:
            copy.wait()

    def move_some(start, stop):
        def one(i, carry):
            move(lax.div(i, npy), lax.rem(i, npy))
            return carry

        lax.fori_loop(start, stop, one, 0)

    out_copies = []
    units = leaves * npy
    marks = [units * m // 8 for m in (0, 5, 6, 7, 8)]
    bout_load.wait()
    for l in range(leaves):
        bmoved[l] = dot(onehot[l], bout[l]).astype(BF16)

    move_some(marks[0], marks[1])
    for copy in far_copies.values():
        copy.wait_send()
    spread(pieces[FIRST:SECOND])

    forwards = []

    def forward(l, h):
        piece = pl.ds(h * step, step)
        for d in range(1, nx):
            x_copies[l, h, d].wait_recv()
            forwards.append(
                send(g.at[0, d, l, piece], g.at[1, d, l, piece], fwd_sem, (l, h, d - 1), twin)
            )

    for copy in tree_loads:
        copy.wait()
    s_copies = {}
    coefs = []
    own = {}
    for t in range(PARTS):
        total = part[0, :, spans[t]]
        for d in range(1, nx):
            for l in range(leaves):
                far_copies[l, t, d].wait_recv()
            total = total + far_in[d, :, spans[t]]
        coefs.append(total)
        ssend[0, spans[t]] = lift(total[0], lt[0]) + lift(total[1], lt[1])
        s_copies[0, t] = send(
            ssend.at[0, spans[t]], srecv.at[0, spans[t]], s_sem, (0, t), sibling(0)
        )
    first_down, second_down, coupled = [], [], {}
    for k in range(levels):
        if k < levels - 1:
            for t in range(PARTS):
                own[t] = lift(ssend[k, spans[t]], ct[0, k])
        if k == 0:
            for t in range(PARTS):
                first_down.append(lower(coefs[t][1], lc[0]))
                second_down.append(lower(coefs[t][0], lc[1]))
        if k == 1:
            spread(pieces[SECOND:THIRD])
        if k < 3:
            move_some(marks[k + 1], marks[k + 2])
        if k < levels - 1:
            w_copies[k].wait_recv()
            for t in range(PARTS):
                s_copies[k, t].wait_recv()
                ssend[k + 1, spans[t]] = own[t] + lift(srecv[k, spans[t]], wsib[k])
                s_copies[k + 1, t] = send(
                    ssend.at[k + 1, spans[t]],
                    srecv.at[k + 1, spans[t]],
                    s_sem,
                    (k + 1, t),
                    sibling(k + 1),
                )
            for t in range(PARTS):
                coupled[k, t] = lower(srecv[k, spans[t]], cc[0, k])
    for l, h in pieces[:FIRST]:
        forward(l, h)
    for l in range(leaves):
        own_copies[l].wait_recv()
        multiply(l, 0, 0, first=True)
        multiply(l, 1, 0)

    ld_copies = {}
    ld_twin = {}
    top = levels - 1
    for t in range(PARTS):
        s_copies[top, t].wait_recv()
        descend = lower(srecv[top, spans[t]], cc[0, top])
        for k in reversed(range(top)):
            descend = coupled[k, t] + lower(descend, ct[0, k])
        ldg[py, 0, spans[t]] = (first_down[t] + lower(descend, lt[0])).astype(BF16)
        ldg[py, 1, spans[t]] = (second_down[t] + lower(descend, lt[1])).astype(BF16)
        block = ldg.at[py, :, spans[t]]
        for d in range(1, nx):
            ld_copies[t, d] = send(block, block, ld_sem, (t, d), peer(d))
        ld_twin[t] = send(block, block, ld_sem, (t, 0), twin)
    spread(pieces[THIRD:])

    for l, h in pieces[FIRST:THIRD]:
        forward(l, h)
    for d in range(1, nx):
        multiply(0, 0, d)
    for copy in forwards[: (nx - 1) * CHUNKS]:
        copy.wait_recv()
    for d in range(1, nx):
        multiply(0, 1, d)

    ld_forwards = []
    for t in range(PARTS):
        for d in range(1, nx):
            ld_copies[t, d].wait_recv()
            block = ldg.at[owner(0, d), :, spans[t]]
            ld_forwards.append(send(block, block, ldf_sem, (t, d - 1), twin))
    for l, h in pieces[THIRD:]:
        forward(l, h)
    for t in range(PARTS):
        ld_twin[t].wait_recv()
    for copy in ld_forwards:
        copy.wait_recv()
    last = leaves - 1
    half = CHUNKS // 2
    for l in range(leaves):
        near[l] += dot_nt(bmoved[l], ldg[:, l].reshape(width, ldg.shape[3]))
        if l < last:
            copy = pltpu.make_async_copy(near.at[l], out.at[l], out_sem.at[l])
            copy.start()
            out_copies.append(copy)
    for start, stop in ((0, half), (half, CHUNKS - 1), (CHUNKS - 1, CHUNKS)):
        first, end = (nx - 1) * (last * CHUNKS + start), (nx - 1) * (last * CHUNKS + stop)
        for copy in forwards[first:end]:
            copy.wait_recv()
        total = near[last]
        for d in range(1, nx):
            for side in range(2):
                total = total + multiply_piece(last, side, d, start, stop)
        near[last] = total
    copy = pltpu.make_async_copy(near.at[last], out.at[last], out_sem.at[last])
    copy.start()
    out_copies.append(copy)

    for copy in sent:
        if not any(copy is other for other in far_copies.values()):
            copy.wait_send()
    for copy in out_copies:
        copy.wait()


def on_device(
    right_sides,
    tree_order,
    dense_blocks,
    basis_out,
    basis_in,
    leaf_transfer,
    leaf_coupling,
    chain_transfer,
    chain_coupling,
):
    npx = lax.axis_size("px")
    npy = lax.axis_size("py")
    levels = npx.bit_length() - 1
    nx = npy // 2
    leaves, rows, width = right_sides.shape
    rank = basis_in.shape[2]
    n = width // npy
    dma = pltpu.SemaphoreType.DMA
    outside = pl.BlockSpec(memory_space=pltpu.HBM)
    scratch = [
        pltpu.VMEM((npy, leaves, rows), jnp.int32),
        pltpu.VMEM((leaves, npy, rows, rows), BF16),
        pltpu.VMEM((leaves, rows, rank), BF16),
        pltpu.VMEM((leaves, rows, rank), BF16),
        pltpu.VMEM(leaf_transfer.shape, BF16),
        pltpu.VMEM(leaf_coupling.shape, BF16),
        pltpu.VMEM(chain_transfer.shape, BF16),
        pltpu.VMEM(chain_coupling.shape, BF16),
        pltpu.VMEM((leaves, rows, rows), BF16),
        pltpu.VMEM((leaves, npy, rows, rows), BF16),
        pltpu.VMEM((leaves, rows, rank), BF16),
        pltpu.VMEM((npy, leaves, n, rank), F32),
        pltpu.VMEM((nx, leaves, n, rank), F32),
        pltpu.VMEM((nx, leaves, n, rank), F32),
        pltpu.VMEM((nx, leaves, n, rank), F32),
        pltpu.VMEM((2, nx, leaves, rows, width), BF16),
        pltpu.VMEM((leaves, rows, width), F32),
        pltpu.VMEM((levels - 1, rank, rank), BF16),
        pltpu.VMEM((levels, n, rank), F32),
        pltpu.VMEM((levels, n, rank), F32),
        pltpu.VMEM((npy, leaves, n, rank), BF16),
        dma((8 + leaves * npy,)),
        dma((leaves,)),
        dma((2, npy - 1)),
        dma((2, levels - 1)),
        dma((2, leaves, nx)),
        dma((2, leaves, PARTS, nx)),
        dma((2, leaves)),
        dma((2, leaves, CHUNKS, nx - 1)),
        dma((2, leaves, CHUNKS, nx - 1)),
        dma((2, levels, PARTS)),
        dma((2, PARTS, nx)),
        dma((2, PARTS, nx - 1)),
    ]
    return pl.pallas_call(
        functools.partial(kernel, npx, npy),
        out_shape=jax.ShapeDtypeStruct((leaves, rows, width), F32),
        in_specs=[outside] * 9,
        out_specs=outside,
        scratch_shapes=scratch,
        compiler_params=pltpu.CompilerParams(
            collective_id=0, has_side_effects=True, vmem_limit_bytes=VMEM
        ),
    )(
        right_sides,
        tree_order,
        dense_blocks,
        basis_out,
        basis_in,
        leaf_transfer,
        leaf_coupling,
        chain_transfer,
        chain_coupling,
    )


def solution(mesh):
    in_specs = (
        P("px", "py", None),
        P("px", "py"),
        P("px", "py", None),
        P("px", "py", None),
        P("px", "py", None),
        P("px", None, None),
        P("px", None, None),
        P("px", None, None, None),
        P("px", None, None, None),
    )
    out_specs = P("px", "py", None)
    return jax.shard_map(
        on_device, mesh=mesh, in_specs=in_specs, out_specs=out_specs, check_vma=False
    )
```

```python
import functools

import jax
import jax.numpy as jnp
from jax import lax
from jax.experimental import pallas as pl
from jax.experimental.pallas import tpu as pltpu
from jax.sharding import PartitionSpec as P

MESH = pl.DeviceIdType.MESH
BF16 = jnp.bfloat16
F32 = jnp.float32
CHUNKS = 4
FIRST, SECOND, THIRD = 1, 5, 7
PARTS = 2
VMEM = 58 * 2**20


def dot(a, b):
    return jnp.dot(a, b, preferred_element_type=F32)


def dot_nt(a, b):
    return lax.dot_general(a, b, (((1,), (1,)), ((), ())), preferred_element_type=F32)


def dot_tn(a, b):
    return lax.dot_general(a, b, (((0,), (0,)), ((), ())), preferred_element_type=F32)


def halves(v):
    high = v.astype(BF16)
    low = (v - high.astype(F32)).astype(BF16)
    return jnp.concatenate([high, low], axis=0)


def lift(v, w):
    t = dot(halves(v), w)
    n = v.shape[0]
    return t[:n] + t[n:]


def lower(v, w):
    t = dot_nt(halves(v), w)
    n = v.shape[0]
    return t[:n] + t[n:]


def kernel(
    npx,
    npy,
    rs_in,
    order_in,
    dense_in,
    bout_in,
    bin_in,
    lt_in,
    lc_in,
    ct_in,
    cc_in,
    out,
    orders,
    dense,
    bout,
    bin_,
    lt,
    lc,
    ct,
    cc,
    onehot,
    moved,
    bmoved,
    coef,
    near_in,
    part,
    far_in,
    g,
    near,
    wsib,
    ssend,
    srecv,
    ldg,
    load_sem,
    out_sem,
    order_sem,
    w_sem,
    near_sem,
    far_sem,
    own_sem,
    x_sem,
    fwd_sem,
    s_sem,
    ld_sem,
    ldf_sem,
):
    levels = npx.bit_length() - 1
    nx = npy // 2
    leaves, rows, width = rs_in.shape
    n = width // npy
    px = lax.axis_index("px")
    py = lax.axis_index("py")
    x = py // 2
    c = py % 2
    twin = {"py": 2 * x + 1 - c}

    def chip(d):
        return lax.rem(x + d + nx, nx)

    def peer(d):
        return {"py": 2 * chip(d) + c}

    def sibling(k):
        bit = (px // 2**k) % 2
        return {"px": px + 2**k * (1 - 2 * bit)}

    def remote(src, dst, sems, index, device):
        return pltpu.make_async_remote_copy(
            src_ref=src,
            dst_ref=dst,
            send_sem=sems.at[(0,) + index],
            recv_sem=sems.at[(1,) + index],
            device_id=device,
            device_id_type=MESH,
        )

    loads = []
    sent = []

    def load(src, dst):
        copy = pltpu.make_async_copy(src, dst, load_sem.at[len(loads)])
        copy.start()
        loads.append(copy)
        return copy

    def send(*args):
        copy = remote(*args)
        copy.start()
        sent.append(copy)
        return copy

    order_load = load(order_in, orders.at[py])
    early = [load(bin_in, bin_), load(rs_in, g.at[0, 0])]
    tree_loads = [load(lt_in, lt), load(ct_in, ct), load(lc_in, lc), load(cc_in, cc)]
    bout_load = load(bout_in, bout)
    dense_loads = [
        [load(dense_in.at[l, :, pl.ds(q * rows, rows)], dense.at[l, q]) for q in range(npy)]
        for l in range(leaves)
    ]

    others = [{"py": lax.rem(py + d, npy)} for d in range(1, npy)]
    partners = others + [sibling(k) for k in range(levels)]
    barrier = pltpu.get_barrier_semaphore()
    for device in partners:
        pl.semaphore_signal(barrier, inc=1, device_id=device, device_id_type=MESH)

    places = lax.broadcasted_iota(jnp.int32, (rows, rows), 0)

    def selection(l, q):
        position = orders[q, pl.ds(l, 1), :] - q * rows
        return jnp.where(places == position, 1.0, 0.0).astype(BF16)

    order_load.wait()
    for l in range(leaves):
        onehot[l] = selection(l, py)
    pl.semaphore_wait(barrier, len(partners))

    step = rows // CHUNKS
    pieces = [(l, h) for l in range(leaves) for h in range(CHUNKS)]
    x_copies = {}

    def spread(wanted):
        for l, h in wanted:
            piece = pl.ds(h * step, step)
            for d in range(1, nx):
                x_copies[l, h, d] = send(
                    rs_in.at[l, piece], g.at[0, d, l, piece], x_sem, (l, h, d - 1), peer(d)
                )

    spread(pieces[:FIRST])
    order_copies = [
        send(orders.at[py], orders.at[py], order_sem, (d,), device)
        for d, device in enumerate(others)
    ]
    w_copies = [
        send(ct_in.at[0, k], wsib.at[k], w_sem, (k,), sibling(k)) for k in range(levels - 1)
    ]

    near_copies = {}
    for copy in early:
        copy.wait()
    for l in range(leaves):
        inward = dot(onehot[l], bin_[l]).astype(BF16)
        values = dot_tn(g[0, 0, l], inward)
        for q in range(npy):
            coef[q, l] = values[q * n : (q + 1) * n]
        for d in list(range(1, nx)) + [0]:
            near_copies[l, d] = send(
                coef.at[2 * chip(d) + 1 - c, l], near_in.at[d, l], near_sem, (l, d), twin
            )
    own_copies = [
        send(rs_in.at[l], g.at[1, 0, l], own_sem, (l,), twin) for l in range(leaves)
    ]

    half = n // PARTS
    spans = [pl.ds(t * half, half) for t in range(PARTS)]
    far_copies = {}
    for l in range(leaves):
        for d in range(1, nx):
            near_copies[l, d].wait_recv()
            q = 2 * chip(d) + c
            part[d, l] = coef[q, l] + near_in[d, l]
            for t in range(PARTS):
                far_copies[l, t, d] = send(
                    part.at[d, l, spans[t]],
                    far_in.at[d, l, spans[t]],
                    far_sem,
                    (l, t, d),
                    peer(d),
                )
    for l in range(leaves):
        near_copies[l, 0].wait_recv()
        part[0, l] = coef[2 * x + c, l] + near_in[0, l]

    def owner(side, d):
        return 2 * chip(-d) + (c if side == 0 else 1 - c)

    def move(l, q):
        turned = dot(onehot[l], dense[l, q]).astype(BF16)
        moved[l, q] = dot_nt(turned, selection(l, q)).astype(BF16)

    def multiply(l, side, d, first=False):
        product = dot(moved[l, owner(side, d)], g[side, d, l])
        near[l] = product if first else near[l] + product

    def multiply_piece(l, side, d, start, stop):
        q = owner(side, d)
        piece = slice(start * step, stop * step)
        return dot(moved[l, q, :, piece], g[side, d, l, piece])

    for copy in order_copies:
        copy.wait_recv()
    for l in range(leaves):
        for copy in dense_loads[l]:
            copy.wait()

    def move_some(start, stop):
        def one(i, carry):
            move(lax.div(i, npy), lax.rem(i, npy))
            return carry

        lax.fori_loop(start, stop, one, 0)

    out_copies = []
    units = leaves * npy
    marks = [units * m // 8 for m in (0, 5, 6, 7, 8)]
    bout_load.wait()
    for l in range(leaves):
        bmoved[l] = dot(onehot[l], bout[l]).astype(BF16)

    move_some(marks[0], marks[0] + units // 4)
    for copy in far_copies.values():
        copy.wait_send()
    spread(pieces[FIRST:SECOND])
    move_some(marks[0] + units // 4, marks[1])

    forwards = []

    def forward(l, h):
        piece = pl.ds(h * step, step)
        for d in range(1, nx):
            x_copies[l, h, d].wait_recv()
            forwards.append(
                send(g.at[0, d, l, piece], g.at[1, d, l, piece], fwd_sem, (l, h, d - 1), twin)
            )

    for copy in tree_loads:
        copy.wait()
    s_copies = {}
    coefs = []
    own = {}
    for t in range(PARTS):
        total = part[0, :, spans[t]]
        for d in range(1, nx):
            for l in range(leaves):
                far_copies[l, t, d].wait_recv()
            total = total + far_in[d, :, spans[t]]
        coefs.append(total)
        ssend[0, spans[t]] = lift(total[0], lt[0]) + lift(total[1], lt[1])
        s_copies[0, t] = send(
            ssend.at[0, spans[t]], srecv.at[0, spans[t]], s_sem, (0, t), sibling(0)
        )
    first_down, second_down, coupled = [], [], {}
    for k in range(levels):
        if k < levels - 1:
            for t in range(PARTS):
                own[t] = lift(ssend[k, spans[t]], ct[0, k])
        if k == 0:
            for t in range(PARTS):
                first_down.append(lower(coefs[t][1], lc[0]))
                second_down.append(lower(coefs[t][0], lc[1]))
        if k == 1:
            spread(pieces[SECOND:THIRD])
        if k < 3:
            move_some(marks[k + 1], marks[k + 2])
        if k < levels - 1:
            w_copies[k].wait_recv()
            for t in range(PARTS):
                s_copies[k, t].wait_recv()
                ssend[k + 1, spans[t]] = own[t] + lift(srecv[k, spans[t]], wsib[k])
                s_copies[k + 1, t] = send(
                    ssend.at[k + 1, spans[t]],
                    srecv.at[k + 1, spans[t]],
                    s_sem,
                    (k + 1, t),
                    sibling(k + 1),
                )
            for t in range(PARTS):
                coupled[k, t] = lower(srecv[k, spans[t]], cc[0, k])
    for l, h in pieces[:FIRST]:
        forward(l, h)
    for l in range(leaves):
        own_copies[l].wait_recv()
        multiply(l, 0, 0, first=True)
        multiply(l, 1, 0)

    ld_copies = {}
    ld_twin = {}
    top = levels - 1
    for t in range(PARTS):
        s_copies[top, t].wait_recv()
        descend = lower(srecv[top, spans[t]], cc[0, top])
        for k in reversed(range(top)):
            descend = coupled[k, t] + lower(descend, ct[0, k])
        ldg[py, 0, spans[t]] = (first_down[t] + lower(descend, lt[0])).astype(BF16)
        ldg[py, 1, spans[t]] = (second_down[t] + lower(descend, lt[1])).astype(BF16)
        block = ldg.at[py, :, spans[t]]
        for d in range(1, nx):
            ld_copies[t, d] = send(block, block, ld_sem, (t, d), peer(d))
        ld_twin[t] = send(block, block, ld_sem, (t, 0), twin)
    spread(pieces[THIRD:])

    for l, h in pieces[FIRST:THIRD]:
        forward(l, h)
    for d in range(1, nx):
        multiply(0, 0, d)
    for copy in forwards[: (nx - 1) * CHUNKS]:
        copy.wait_recv()
    for d in range(1, nx):
        multiply(0, 1, d)

    ld_forwards = []
    for t in range(PARTS):
        for d in range(1, nx):
            ld_copies[t, d].wait_recv()
            block = ldg.at[owner(0, d), :, spans[t]]
            ld_forwards.append(send(block, block, ldf_sem, (t, d - 1), twin))
    for l, h in pieces[THIRD:]:
        forward(l, h)
    for t in range(PARTS):
        ld_twin[t].wait_recv()
    for copy in ld_forwards:
        copy.wait_recv()
    last = leaves - 1
    half = CHUNKS // 2
    for l in range(leaves):
        near[l] += dot_nt(bmoved[l], ldg[:, l].reshape(width, ldg.shape[3]))
        if l < last:
            copy = pltpu.make_async_copy(near.at[l], out.at[l], out_sem.at[l])
            copy.start()
            out_copies.append(copy)
    for start, stop in ((0, half), (half, CHUNKS - 1), (CHUNKS - 1, CHUNKS)):
        first, end = (nx - 1) * (last * CHUNKS + start), (nx - 1) * (last * CHUNKS + stop)
        for copy in forwards[first:end]:
            copy.wait_recv()
        total = near[last]
        for d in range(1, nx):
            for side in range(2):
                total = total + multiply_piece(last, side, d, start, stop)
        near[last] = total
    copy = pltpu.make_async_copy(near.at[last], out.at[last], out_sem.at[last])
    copy.start()
    out_copies.append(copy)

    for copy in sent:
        if not any(copy is other for other in far_copies.values()):
            copy.wait_send()
    for copy in out_copies:
        copy.wait()


def on_device(
    right_sides,
    tree_order,
    dense_blocks,
    basis_out,
    basis_in,
    leaf_transfer,
    leaf_coupling,
    chain_transfer,
    chain_coupling,
):
    npx = lax.axis_size("px")
    npy = lax.axis_size("py")
    levels = npx.bit_length() - 1
    nx = npy // 2
    leaves, rows, width = right_sides.shape
    rank = basis_in.shape[2]
    n = width // npy
    dma = pltpu.SemaphoreType.DMA
    outside = pl.BlockSpec(memory_space=pltpu.HBM)
    scratch = [
        pltpu.VMEM((npy, leaves, rows), jnp.int32),
        pltpu.VMEM((leaves, npy, rows, rows), BF16),
        pltpu.VMEM((leaves, rows, rank), BF16),
        pltpu.VMEM((leaves, rows, rank), BF16),
        pltpu.VMEM(leaf_transfer.shape, BF16),
        pltpu.VMEM(leaf_coupling.shape, BF16),
        pltpu.VMEM(chain_transfer.shape, BF16),
        pltpu.VMEM(chain_coupling.shape, BF16),
        pltpu.VMEM((leaves, rows, rows), BF16),
        pltpu.VMEM((leaves, npy, rows, rows), BF16),
        pltpu.VMEM((leaves, rows, rank), BF16),
        pltpu.VMEM((npy, leaves, n, rank), F32),
        pltpu.VMEM((nx, leaves, n, rank), F32),
        pltpu.VMEM((nx, leaves, n, rank), F32),
        pltpu.VMEM((nx, leaves, n, rank), F32),
        pltpu.VMEM((2, nx, leaves, rows, width), BF16),
        pltpu.VMEM((leaves, rows, width), F32),
        pltpu.VMEM((levels - 1, rank, rank), BF16),
        pltpu.VMEM((levels, n, rank), F32),
        pltpu.VMEM((levels, n, rank), F32),
        pltpu.VMEM((npy, leaves, n, rank), BF16),
        dma((8 + leaves * npy,)),
        dma((leaves,)),
        dma((2, npy - 1)),
        dma((2, levels - 1)),
        dma((2, leaves, nx)),
        dma((2, leaves, PARTS, nx)),
        dma((2, leaves)),
        dma((2, leaves, CHUNKS, nx - 1)),
        dma((2, leaves, CHUNKS, nx - 1)),
        dma((2, levels, PARTS)),
        dma((2, PARTS, nx)),
        dma((2, PARTS, nx - 1)),
    ]
    return pl.pallas_call(
        functools.partial(kernel, npx, npy),
        out_shape=jax.ShapeDtypeStruct((leaves, rows, width), F32),
        in_specs=[outside] * 9,
        out_specs=outside,
        scratch_shapes=scratch,
        compiler_params=pltpu.CompilerParams(
            collective_id=0, has_side_effects=True, vmem_limit_bytes=VMEM
        ),
    )(
        right_sides,
        tree_order,
        dense_blocks,
        basis_out,
        basis_in,
        leaf_transfer,
        leaf_coupling,
        chain_transfer,
        chain_coupling,
    )


def solution(mesh):
    in_specs = (
        P("px", "py", None),
        P("px", "py"),
        P("px", "py", None),
        P("px", "py", None),
        P("px", "py", None),
        P("px", None, None),
        P("px", None, None),
        P("px", None, None, None),
        P("px", None, None, None),
    )
    out_specs = P("px", "py", None)
    return jax.shard_map(
        on_device, mesh=mesh, in_specs=in_specs, out_specs=out_specs, check_vma=False
    )
```
